32 devices in a mesh: group: 2 (over y), ctr: 4 (over x, core), dp: 4 (over z).
Axes of the slice: x: 2, y: 2, z: 4, core: 2. Of those that a mesh axis runs over, the one named last changes fastest.
Arguments:
- points: bfloat16 [32768, 256], P(('group', 'ctr', 'dp')), parts along dimension 0, may hold values from -6 to 6
- labels: bfloat16 [32768], P(('group', 'ctr', 'dp')), parts along dimension 0, may hold values from 0 to 2
- centre_index: int32 [1024], P(('group', 'ctr', 'dp')), parts along dimension 0, may hold values from 0 to 16383, as said below
- kernel_factor: float32 [1024, 512], P(('group', 'ctr')), parts along dimension 0, as said below
- ridge_factor: float32 [1024, 512], P(('group', 'ctr')), parts along dimension 0, as said below
Outputs:
- fitted: float32 [32768], P(('group', 'ctr', 'dp')), parts along dimension 0
The draws below stay inside these ranges and needn't reach their ends.
There are 2 independent parts, one for each index of `group`. The reference program is written for one: setup_inputs(seed, part) draws one part's arguments, and reference() takes and returns one part's arrays. A program takes and returns all parts, laid end to end along the dimension named above; each array names one. Nothing has to cross between parts.
Inputs may be any that keep to these rules, and one draw needn't show every extreme that they name: `centre_index`: entry k lies in rows k * 32 to k * 32 + 31 of points. `kernel_factor`: upper triangular with a positive diagonal. `ridge_factor`: upper triangular with a positive diagonal.
All inputs are finite; a program needn't handle non-finite values.
Results may differ from the reference program's by a relative error of at most 0.004.
Values may be sent and summed in bfloat16 or wider, within the bound.
A program may use at most 64 MiB of HBM per device.

```python
import jax
import jax.numpy as jnp
from jax import lax

D = 256
NP = 1024
CB = 128
ITERS = 2
NPTS = 16384
M = 512
N_DP = 4


def triangle(key, off_values, lowest, highest):
    row_place = jnp.arange(M)[:, None]
    column = jnp.arange(M)[None, :]
    diagonal = jax.random.uniform(jax.random.fold_in(key, 1), (M, 1), jnp.float32, lowest, highest)
    return jnp.where(column == row_place, diagonal, jnp.where(column > row_place, off_values, 0.0)).astype(jnp.float32)


def draw_kernel_factor(key, part):
    key = jax.random.fold_in(key, 11)
    off_values = jax.random.uniform(key, (M, M), jnp.float32, -1.0, 1.0) * (0.25 / M ** 0.5)
    return triangle(key, off_values, 0.25, 0.4)


def draw_ridge_factor(key, part):
    key = jax.random.fold_in(key, 23)
    off_values = jax.random.uniform(key, (M, M), jnp.float32, -1.0, 1.0) * (0.25 / M ** 0.5)
    return triangle(key, off_values, 0.33, 0.5)


def draw_centre_index(key, part):
    key = jax.random.fold_in(key, 7)
    per_device = CB // N_DP
    stride = NP // per_device
    entries = jnp.arange(M)
    device = entries // per_device
    position = entries % per_device
    offset = jax.random.randint(key, (M,), 0, stride)
    offset = jnp.where(entries == 0, 0, offset)
    offset = jnp.where(entries == M - 1, stride - 1, offset)
    return (device * NP + position * stride + offset).astype(jnp.int32)


def steps_of(key, shape, pieces, least, high):
    def one(axis_at, blocks):
        steps = jax.random.uniform(jax.random.fold_in(jax.random.fold_in(key, 6), axis_at), (blocks,), jnp.float32, least / len(pieces), high / len(pieces))
        return jnp.repeat(jnp.exp(steps), shape[axis_at] // blocks).reshape((-1,) + (1,) * (len(shape) - axis_at - 1))

    level = one(*pieces[0])
    for cut in pieces[1:]:
        level = level * one(*cut)
    return level


def gaussian(key, dims, deviation, reach, shards=(), kind=jnp.bfloat16):
    array = deviation * jax.random.normal(key, dims, jnp.float32)
    if shards:
        array = array * steps_of(key, dims, shards, -0.22, 0.18)
    return jnp.clip(array, -reach, reach).astype(kind)


def setup_inputs(seed: int = 0, part: int = 0) -> dict:
    key_list = jax.random.split(jax.random.key(seed), 6)
    part_keys = jax.random.split(jax.random.fold_in(key_list[5], part), 6)
    return {
        "points": gaussian(part_keys[0], (NPTS, D), 1.0, 6.0, ((0, 16),)),
        "labels": jnp.clip(2.0 * jax.random.uniform(part_keys[1], (NPTS,), jnp.float32) ** steps_of(part_keys[1], (NPTS,), ((0, 16),), -0.2, 0.2), 0.0, 2.0).astype(jnp.bfloat16),
        "centre_index": draw_centre_index(jax.random.fold_in(jax.random.fold_in(key_list[5], part), 71), part),
        "kernel_factor": draw_kernel_factor(jax.random.fold_in(jax.random.fold_in(key_list[5], part), 71), part),
        "ridge_factor": draw_ridge_factor(jax.random.fold_in(jax.random.fold_in(key_list[5], part), 71), part),
    }


ridge_weight = 1.0e-3


def kernel_block(point_rows, centres):
    feature_count = point_rows.shape[1]
    point_wide = point_rows.astype(jnp.float32)
    centre_wide = centres.astype(jnp.float32)
    point_sq = jnp.sum(point_wide * point_wide, axis=1)
    centre_sq = jnp.sum(centre_wide * centre_wide, axis=1)
    products = jnp.dot(point_rows, centres.T, preferred_element_type=jnp.float32)
    exponent = (2.0 * products - point_sq[:, None] - centre_sq[None, :]) * (2.0 / feature_count)
    return jnp.exp(exponent).astype(jnp.bfloat16)


def block_solve(factor, vector, transposed):
    if transposed:
        return jnp.dot(vector, factor, precision=lax.Precision.HIGHEST)
    return jnp.dot(factor, vector, precision=lax.Precision.HIGHEST)


def label_pass(point_blocks, label_blocks, centres):
    def add_block(running, inputs):
        rows_now, labels_now = inputs
        return running + jnp.dot(labels_now, kernel_block(rows_now, centres), preferred_element_type=jnp.float32), None

    result, unused = lax.scan(add_block, jnp.zeros((centres.shape[0],), jnp.float32), (point_blocks, label_blocks))
    return result


def both_pass(point_blocks, centres, vector):
    def add_block(running, rows_now):
        kernel = kernel_block(rows_now, centres)
        mapped = jnp.dot(kernel, vector, preferred_element_type=jnp.float32).astype(jnp.bfloat16)
        return running + jnp.dot(mapped, kernel, preferred_element_type=jnp.float32), None

    result, unused = lax.scan(add_block, jnp.zeros((centres.shape[0],), jnp.float32), point_blocks)
    return result


def forward_pass(point_blocks, centres, vector):
    values = lax.map(lambda rows_now: jnp.dot(kernel_block(rows_now, centres), vector, preferred_element_type=jnp.float32), point_blocks)
    return values.reshape(-1)


def reference(points, labels, centre_index, kernel_factor, ridge_factor):
    centres = jnp.take(points, centre_index, axis=0)
    point_blocks = points.reshape(-1, NP, D)
    label_blocks = labels.reshape(-1, NP)
    all_points = points.shape[0]

    def precondition(vector):
        scaled = block_solve(ridge_factor, vector, False)
        return scaled, block_solve(kernel_factor, scaled, False)

    def operator(vector):
        scaled, lifted = precondition(vector)
        summed = both_pass(point_blocks, centres, lifted.astype(jnp.bfloat16))
        inner_side = block_solve(kernel_factor, summed, True) / all_points + ridge_weight * scaled
        return block_solve(ridge_factor, inner_side, True)

    projected = label_pass(point_blocks, label_blocks, centres)
    right_side = block_solve(ridge_factor, block_solve(kernel_factor, projected, True) / all_points, True)
    solution = jnp.zeros_like(right_side)
    residual = right_side
    direction = right_side
    norm_now = jnp.sum(residual * residual)
    for iteration in range(ITERS):
        mapped = operator(direction)
        step_size = norm_now / jnp.sum(direction * mapped)
        solution = solution + step_size * direction
        residual = residual - step_size * mapped
        norm_next = jnp.sum(residual * residual)
        direction = residual + (norm_next / norm_now) * direction
        norm_now = norm_next
    unused, coefficients = precondition(solution)
    return forward_pass(point_blocks, centres, coefficients.astype(jnp.bfloat16))
```

```python
import functools

import jax
import jax.numpy as jnp
from jax import lax
from jax.experimental import pallas as pl
from jax.experimental.pallas import tpu as pltpu
from jax.sharding import PartitionSpec as P

ITERS = 2
RIDGE = 0.001
MESH = pl.DeviceIdType.MESH
F32 = jnp.float32
BF16 = jnp.bfloat16
NT = (((1,), (1,)), ((), ()))


def kernel(nc, nd, pts, lab, idx, kf, rf, out,
           cbuf, kt, rbuf, tbuf, zbuf, xbuf,
           c1s, c1r, c2s, c2r, fs, fr, zs, zr, xs, xr):
    n_pts, feats = pts.shape
    per = idx.shape[1]
    half = feats // 2
    cb = per * nd
    m = cb * nc
    all_points = float(n_pts * nc * nd)
    c = lax.axis_index("ctr")
    d = lax.axis_index("dp")

    barrier = pltpu.get_barrier_semaphore()
    for k in range(1, nd):
        pl.semaphore_signal(barrier, inc=1, device_id={"dp": lax.rem(d + k, nd)}, device_id_type=MESH)
    for k in range(1, nc):
        pl.semaphore_signal(barrier, inc=1, device_id={"ctr": lax.rem(c + k, nc)}, device_id_type=MESH)

    first = (c * nd + d) * n_pts
    local = (idx[...] - first).astype(F32)
    square = lax.broadcasted_iota(jnp.int32, (per, per), 0) == lax.broadcasted_iota(jnp.int32, (per, per), 1)
    local = jnp.sum(jnp.where(square, local, 0.0), axis=1, keepdims=True).astype(jnp.int32)
    places = lax.broadcasted_iota(jnp.int32, (per, n_pts), 1)
    onehot = jnp.where(places == local, 1.0, 0.0).astype(BF16)
    chosen = jnp.dot(onehot, pts[...], preferred_element_type=F32)
    cbuf[c, d] = jnp.concatenate([chosen[:, :half], chosen[:, half:]], axis=0).astype(BF16)

    rbuf[c] = rf[...]
    tbuf[c] = kf[...].T

    pl.semaphore_wait(barrier, nc + nd - 2)

    def spread(ref_src, axis, me, n, send, recv):
        copies = []
        for k in range(1, n):
            copy = pltpu.make_async_remote_copy(
                src_ref=ref_src, dst_ref=ref_src, send_sem=send.at[k - 1], recv_sem=recv.at[k - 1],
                device_id={axis: lax.rem(me + k, n)}, device_id_type=MESH)
            copy.start()
            copies.append(copy)
        return copies

    sent = []
    first_copies = spread(cbuf.at[c, d], "dp", d, nd, c1s, c1r)
    sent += first_copies

    def factor_copies(cc):
        made = []
        for k in range(1, nc):
            peer = (cc + k) % nc
            for which, ref in ((0, tbuf.at[cc, pl.ds(cb * cc, m - cb * cc)]),
                               (1, rbuf.at[cc, :, pl.ds(cb * cc, m - cb * cc)])):
                made.append(pltpu.make_async_remote_copy(
                    src_ref=ref, dst_ref=ref, send_sem=fs.at[which, k - 1], recv_sem=fr.at[which, k - 1],
                    device_id={"ctr": peer}, device_id_type=MESH))
        return made

    def factor_sources(cc):
        made = []
        for k in range(1, nc):
            src = (cc - k) % nc
            for which, ref in ((0, tbuf.at[src, pl.ds(cb * src, m - cb * src)]),
                               (1, rbuf.at[src, :, pl.ds(cb * src, m - cb * src)])):
                made.append(pltpu.make_async_remote_copy(
                    src_ref=ref, dst_ref=ref, send_sem=fs.at[which, k - 1], recv_sem=fr.at[which, k - 1],
                    device_id={"ctr": src}, device_id_type=MESH))
        return made

    wide = pts[...].astype(F32)
    sq = wide * wide
    sq_hi = sq.astype(BF16)
    sq_lo = (sq - sq_hi.astype(F32)).astype(BF16)
    ones = jnp.ones((8, feats), BF16)
    point_sq = (lax.dot_general(ones, sq_hi, NT, preferred_element_type=F32)
                + lax.dot_general(ones, sq_lo, NT, preferred_element_type=F32))[:1]

    for copy in first_copies:
        copy.wait_recv()
    second_copies = spread(cbuf.at[c], "ctr", c, nc, c2s, c2r)
    sent += second_copies

    for cc in range(nc):
        @pl.when(c == cc)
        def _(cc=cc):
            for copy in factor_copies(cc):
                copy.start()

    def form(owner):
        block = cbuf[owner].astype(F32).reshape(nd, 2, per, half)
        left = block[:, 0].reshape(cb, half)
        right = block[:, 1].reshape(cb, half)
        centre_sq = jnp.sum(left * left + right * right, axis=1, keepdims=True)
        centres = jnp.concatenate([left, right], axis=1).astype(BF16)
        products = lax.dot_general(centres, pts[...], NT, preferred_element_type=F32)
        exponent = (2.0 * products - point_sq - centre_sq) * (2.0 / feats)
        kt[pl.ds(pl.multiple_of(owner * cb, cb), cb), :] = jnp.exp(exponent).astype(BF16)

    form(c)
    for k in range(1, nc):
        second_copies[k - 1].wait_recv()
        form(lax.rem(c - k + nc, nc))

    def total(r, part):
        zbuf[r, d] = part
        copies = spread(zbuf.at[r, d], "dp", d, nd, zs.at[r], zr.at[r])
        for copy in copies:
            copy.wait_recv()
        acc = zbuf[r, 0]
        for k in range(1, nd):
            acc = acc + zbuf[r, k]
        xbuf[r, c] = acc
        more = spread(xbuf.at[r, c], "ctr", c, nc, xs.at[r], xr.at[r])
        for copy in more:
            copy.wait_recv()
        acc = xbuf[r, 0]
        for k in range(1, nc):
            acc = acc + xbuf[r, k]
        sent.extend(copies + more)
        return acc

    def ridge_solve(row):
        return [jnp.sum(rbuf[b, :, cb * b:] * row[:, cb * b:], axis=1, keepdims=True) for b in range(nc)]

    def ridge_solve_transposed(column):
        parts = [0.0] * nc
        for b in range(nc):
            for j in range(b, nc):
                prod = rbuf[b, :, cb * j:cb * (j + 1)] * column[b]
                parts[j] = parts[j] + prod
        return jnp.concatenate([jnp.sum(p, axis=0, keepdims=True) for p in parts], axis=1)

    def kernel_solve(column):
        rows = []
        for b in range(nc):
            acc = 0.0
            for j in range(b, nc):
                acc = acc + tbuf[b, cb * j:cb * (j + 1), :] * column[j]
            rows.append(jnp.sum(acc, axis=0, keepdims=True))
        return jnp.concatenate(rows, axis=1)

    def kernel_solve_transposed(row):
        columns = []
        for j in range(nc):
            acc = 0.0
            for b in range(j + 1):
                acc = acc + tbuf[b, cb * j:cb * (j + 1), :] * row[:, cb * b:cb * (b + 1)]
            columns.append(jnp.sum(acc, axis=1, keepdims=True))
        return columns

    def to_centres(row):
        return lax.dot_general(row, kt[...], NT, preferred_element_type=F32)

    def to_points(row):
        return jnp.dot(row, kt[...], preferred_element_type=F32)

    summed = total(0, to_centres(lab[...]))
    for cc in range(nc):
        @pl.when(c == cc)
        def _(cc=cc):
            for copy in factor_sources(cc):
                copy.wait_recv()
    right_side = ridge_solve_transposed(kernel_solve_transposed(summed / all_points))
    beta = jnp.zeros_like(right_side)
    residual = right_side
    direction = right_side
    norm_now = jnp.sum(residual * residual, axis=1, keepdims=True)
    for iteration in range(ITERS):
        scaled = ridge_solve(direction)
        lifted = kernel_solve(scaled).astype(BF16)
        image = to_points(lifted).astype(BF16)
        summed = total(1 + iteration, to_centres(image))
        inner = kernel_solve_transposed(summed / all_points)
        mapped = ridge_solve_transposed([a + RIDGE * s for a, s in zip(inner, scaled)])
        step = norm_now / jnp.sum(direction * mapped, axis=1, keepdims=True)
        beta = beta + step * direction
        residual = residual - step * mapped
        norm_next = jnp.sum(residual * residual, axis=1, keepdims=True)
        direction = residual + (norm_next / norm_now) * direction
        norm_now = norm_next
    coefficients = kernel_solve(ridge_solve(beta)).astype(BF16)
    out[...] = to_points(coefficients)

    for copy in sent:
        copy.wait_send()
    for cc in range(nc):
        @pl.when(c == cc)
        def _(cc=cc):
            for copy in factor_copies(cc):
                copy.wait_send()


def solution(mesh):
    nc, nd = mesh.shape["ctr"], mesh.shape["dp"]

    def body(points, labels, centre_index, kernel_factor, ridge_factor):
        n_pts, feats = points.shape
        per = centre_index.shape[0]
        cb = kernel_factor.shape[0]
        m = cb * nc
        dma = pltpu.SemaphoreType.DMA
        rounds = ITERS + 1
        fitted = pl.pallas_call(
            functools.partial(kernel, nc, nd),
            out_shape=jax.ShapeDtypeStruct((1, n_pts), F32),
            in_specs=[pl.BlockSpec(memory_space=pltpu.VMEM)] * 5,
            out_specs=pl.BlockSpec(memory_space=pltpu.VMEM),
            scratch_shapes=[
                pltpu.VMEM((nc, nd, 2 * per, feats // 2), BF16),
                pltpu.VMEM((m, n_pts), BF16),
                pltpu.VMEM((nc, cb, m), F32),
                pltpu.VMEM((nc, m, cb), F32),
                pltpu.VMEM((rounds, nd, 1, m), F32),
                pltpu.VMEM((rounds, nc, 1, m), F32),
                dma((nd - 1,)), dma((nd - 1,)),
                dma((nc - 1,)), dma((nc - 1,)),
                dma((2, nc - 1)), dma((2, nc - 1)),
                dma((rounds, nd - 1)), dma((rounds, nd - 1)),
                dma((rounds, nc - 1)), dma((rounds, nc - 1)),
            ],
            compiler_params=pltpu.CompilerParams(
                collective_id=0, has_side_effects=True, vmem_limit_bytes=56 * 2**20),
        )(points, labels.reshape(1, -1), centre_index.reshape(1, -1), kernel_factor, ridge_factor)
        return fitted.reshape(-1)

    whole = ("group", "ctr", "dp")
    in_specs = (P(whole, None), P(whole), P(whole), P(("group", "ctr"), None), P(("group", "ctr"), None))
    return jax.shard_map(body, mesh=mesh, in_specs=in_specs, out_specs=P(whole), check_vma=False)
```

```python
import functools

import jax
import jax.numpy as jnp
from jax import lax
from jax.experimental import pallas as pl
from jax.experimental.pallas import tpu as pltpu
from jax.sharding import PartitionSpec as P

ITERS = 2
RIDGE = 0.001
MESH = pl.DeviceIdType.MESH
F32 = jnp.float32
BF16 = jnp.bfloat16
NT = (((1,), (1,)), ((), ()))


def kernel(nc, nd, flat, pts_in, lab_in, idx_in, kf_in, rf_in, out,
           pts, lab, idx, kf, cbuf, kt, rbuf, tbuf, zbuf, xbuf,
           ins, c1s, c1r, c2s, c2r, fs, fr, zs, zr, xs, xr):
    n_pts, feats = pts.shape
    per = idx.shape[1]
    half = feats // 2
    cb = per * nd
    m = cb * nc
    all_points = float(n_pts * nc * nd)
    c = lax.axis_index("ctr")
    d = lax.axis_index("dp")

    others = [(kc, kd) for kc in range(nc) for kd in range(nd) if (kc or kd) and (flat or not (kc and kd))]
    barrier = pltpu.get_barrier_semaphore()
    for kc, kd in others:
        pl.semaphore_signal(barrier, inc=1, device_id_type=MESH,
                            device_id={"ctr": lax.rem(c + kc, nc), "dp": lax.rem(d + kd, nd)})
    loads = [pltpu.make_async_copy(a, b, ins.at[i]) for i, (a, b) in enumerate(
        ((idx_in, idx), (pts_in, pts), (kf_in, kf), (rf_in, rbuf.at[c]), (lab_in, lab)))]
    for load in loads:
        load.start()

    first = (c * nd + d) * n_pts
    loads[0].wait()
    loads[1].wait()
    local = (idx[...] - first).astype(F32)
    square = lax.broadcasted_iota(jnp.int32, (per, per), 0) == lax.broadcasted_iota(jnp.int32, (per, per), 1)
    local = jnp.sum(jnp.where(square, local, 0.0), axis=1, keepdims=True).astype(jnp.int32)
    places = lax.broadcasted_iota(jnp.int32, (per, n_pts), 1)
    onehot = jnp.where(places == local, 1.0, 0.0).astype(BF16)
    chosen = jnp.dot(onehot, pts[...], preferred_element_type=F32)
    cbuf[c, d] = jnp.concatenate([chosen[:, :half], chosen[:, half:]], axis=0).astype(BF16)

    loads[2].wait()
    tbuf[c] = kf[...].T
    loads[3].wait()
    loads[4].wait()

    pl.semaphore_wait(barrier, len(others))

    def spread(ref_src, axis, me, n, send, recv):
        copies = []
        for k in range(1, n):
            copy = pltpu.make_async_remote_copy(
                src_ref=ref_src, dst_ref=ref_src, send_sem=send.at[k - 1], recv_sem=recv.at[k - 1],
                device_id={axis: lax.rem(me + k, n)}, device_id_type=MESH)
            copy.start()
            copies.append(copy)
        return copies

    sent = []
    first_copies = spread(cbuf.at[c, d], "dp", d, nd, c1s, c1r)
    sent += first_copies

    def factor_copy(which, block, to, send):
        rest = pl.ds(cb * block, m - cb * block)
        ref = rbuf.at[block, :, rest] if which else tbuf.at[block, rest]
        return pltpu.make_async_remote_copy(
            src_ref=ref, dst_ref=ref, send_sem=fs.at[which, send], recv_sem=fr.at[which, block],
            device_id={"ctr": to}, device_id_type=MESH)

    def same_core(cc):
        return [(cc + k) % nc for k in range(2, nc, 2)]

    def direct(cc, which):
        return [factor_copy(which, cc, p, p) for p in same_core(cc) + [cc ^ 1]]

    def handed(cc, which):
        return [factor_copy(which, p, cc ^ 1, nc + p) for p in same_core(cc)]

    def arriving(cc, which):
        return [factor_copy(which, p, p, p) for p in same_core(cc ^ 1) + [cc ^ 1]]

    def on_each(action):
        for cc in range(nc):
            pl.when(c == cc)(functools.partial(action, cc))

    def factors_start(cc):
        for which in range(2):
            for copy in direct(cc, which):
                copy.start()

    def factors_hand_on(cc):
        for which in range(2):
            for p in same_core(cc):
                factor_copy(which, p, p, p).wait_recv()
            for copy in handed(cc, which):
                copy.start()

    def factors_arrive(which, cc):
        for copy in arriving(cc, which):
            copy.wait_recv()

    def factors_end(cc):
        for which in range(2):
            for copy in direct(cc, which) + handed(cc, which):
                copy.wait_send()

    wide = pts[...].astype(F32)
    sq = wide * wide
    sq_hi = sq.astype(BF16)
    sq_lo = (sq - sq_hi.astype(F32)).astype(BF16)
    ones = jnp.ones((8, feats), BF16)
    point_sq = (lax.dot_general(ones, sq_hi, NT, preferred_element_type=F32)
                + lax.dot_general(ones, sq_lo, NT, preferred_element_type=F32))[:1]

    for copy in first_copies:
        copy.wait_recv()
    second_copies = spread(cbuf.at[c], "ctr", c, nc, c2s, c2r)
    sent += second_copies

    on_each(factors_start)

    def form(owner):
        block = cbuf[owner].astype(F32).reshape(nd, 2, per, half)
        left = block[:, 0].reshape(cb, half)
        right = block[:, 1].reshape(cb, half)
        centre_sq = jnp.sum(left * left + right * right, axis=1, keepdims=True)
        centres = jnp.concatenate([left, right], axis=1).astype(BF16)
        products = lax.dot_general(centres, pts[...], NT, preferred_element_type=F32)
        exponent = (2.0 * products - point_sq - centre_sq) * (2.0 / feats)
        kt[pl.ds(pl.multiple_of(owner * cb, cb), cb), :] = jnp.exp(exponent).astype(BF16)

    form(c)
    for k in range(1, nc):
        second_copies[k - 1].wait_recv()
        form(lax.rem(c - k + nc, nc))

    def total(r, part, meanwhile=None):
        if flat:
            zbuf[r, c, d] = part
            copies = []
            for i, (kc, kd) in enumerate(others):
                copy = pltpu.make_async_remote_copy(
                    src_ref=zbuf.at[r, c, d], dst_ref=zbuf.at[r, c, d],
                    send_sem=zs.at[r, i], recv_sem=zr.at[r, i], device_id_type=MESH,
                    device_id={"ctr": lax.rem(c + kc, nc), "dp": lax.rem(d + kd, nd)})
                copy.start()
                copies.append(copy)
            if meanwhile is not None:
                meanwhile()
            for copy in copies:
                copy.wait_recv()
            sent.extend(copies)
            return jnp.sum(zbuf[r].reshape(nc * nd, m), axis=0, keepdims=True)
        zbuf[r, 0, d] = part
        copies = spread(zbuf.at[r, 0, d], "dp", d, nd, zs.at[r], zr.at[r])
        for copy in copies:
            copy.wait_recv()
        xbuf[r, c] = jnp.sum(zbuf[r, 0].reshape(nd, m), axis=0, keepdims=True)
        more = spread(xbuf.at[r, c], "ctr", c, nc, xs.at[r], xr.at[r])
        if meanwhile is not None:
            meanwhile()
        for copy in more:
            copy.wait_recv()
        sent.extend(copies + more)
        return jnp.sum(xbuf[r].reshape(nc, m), axis=0, keepdims=True)

    def ridge_solve(row):
        return [jnp.sum(rbuf[b, :, cb * b:] * row[:, cb * b:], axis=1, keepdims=True) for b in range(nc)]

    def ridge_solve_transposed(column):
        parts = [0.0] * nc
        for b in range(nc):
            for j in range(b, nc):
                prod = rbuf[b, :, cb * j:cb * (j + 1)] * column[b]
                parts[j] = parts[j] + prod
        return jnp.concatenate([jnp.sum(p, axis=0, keepdims=True) for p in parts], axis=1)

    def kernel_solve(column):
        rows = []
        for b in range(nc):
            acc = 0.0
            for j in range(b, nc):
                acc = acc + tbuf[b, cb * j:cb * (j + 1), :] * column[j]
            rows.append(jnp.sum(acc, axis=0, keepdims=True))
        return jnp.concatenate(rows, axis=1)

    def kernel_solve_transposed(row):
        columns = []
        for j in range(nc):
            acc = 0.0
            for b in range(j + 1):
                acc = acc + tbuf[b, cb * j:cb * (j + 1), :] * row[:, cb * b:cb * (b + 1)]
            columns.append(jnp.sum(acc, axis=1, keepdims=True))
        return columns

    def to_centres(row):
        return lax.dot_general(row, kt[...], NT, preferred_element_type=F32)

    def to_points(row):
        return jnp.dot(row, kt[...], preferred_element_type=F32)

    label_row = jnp.concatenate([lab[r:r + 1, :] for r in range(n_pts // 128)], axis=1)
    summed = total(0, to_centres(label_row), lambda: on_each(factors_hand_on))
    on_each(functools.partial(factors_arrive, 0))
    lowered = kernel_solve_transposed(summed / all_points)
    on_each(functools.partial(factors_arrive, 1))
    right_side = ridge_solve_transposed(lowered)
    beta = jnp.zeros_like(right_side)
    residual = right_side
    direction = right_side
    norm_now = jnp.sum(residual * residual, axis=1, keepdims=True)
    for iteration in range(ITERS):
        scaled = ridge_solve(direction)
        lifted = kernel_solve(scaled).astype(BF16)
        image = to_points(lifted).astype(BF16)
        summed = total(1 + iteration, to_centres(image))
        inner = kernel_solve_transposed(summed / all_points)
        mapped = ridge_solve_transposed([a + RIDGE * s for a, s in zip(inner, scaled)])
        step = norm_now / jnp.sum(direction * mapped, axis=1, keepdims=True)
        beta = beta + step * direction
        residual = residual - step * mapped
        norm_next = jnp.sum(residual * residual, axis=1, keepdims=True)
        direction = residual + (norm_next / norm_now) * direction
        norm_now = norm_next
    coefficients = kernel_solve(ridge_solve(beta)).astype(BF16)
    out[...] = to_points(coefficients)

    for copy in sent:
        copy.wait_send()
    on_each(factors_end)


def solution(mesh):
    nc, nd = mesh.shape["ctr"], mesh.shape["dp"]

    def body(points, labels, centre_index, kernel_factor, ridge_factor):
        n_pts, feats = points.shape
        per = centre_index.shape[0]
        cb = kernel_factor.shape[0]
        m = cb * nc
        dma = pltpu.SemaphoreType.DMA
        rounds = ITERS + 1
        flat = nc * nd <= 32
        rows = nc if flat else 1
        links = nc * nd - 1 if flat else nd - 1
        fitted = pl.pallas_call(
            functools.partial(kernel, nc, nd, flat),
            out_shape=jax.ShapeDtypeStruct((1, n_pts), F32),
            in_specs=[pl.BlockSpec(memory_space=pl.ANY)] * 5,
            out_specs=pl.BlockSpec(memory_space=pltpu.VMEM),
            scratch_shapes=[
                pltpu.VMEM((n_pts, feats), BF16),
                pltpu.VMEM((n_pts // 128, 128), BF16),
                pltpu.VMEM((1, per), jnp.int32),
                pltpu.VMEM((cb, m), F32),
                pltpu.VMEM((nc, nd, 2 * per, feats // 2), BF16),
                pltpu.VMEM((m, n_pts), BF16),
                pltpu.VMEM((nc, cb, m), F32),
                pltpu.VMEM((nc, m, cb), F32),
                pltpu.VMEM((rounds, rows, nd, 1, m), F32),
                pltpu.VMEM((rounds, nc, 1, m), F32),
                dma((5,)),
                dma((nd - 1,)), dma((nd - 1,)),
                dma((nc - 1,)), dma((nc - 1,)),
                dma((2, 2 * nc)), dma((2, nc)),
                dma((rounds, links)), dma((rounds, links)),
                dma((rounds, nc - 1)), dma((rounds, nc - 1)),
            ],
            compiler_params=pltpu.CompilerParams(
                collective_id=0, has_side_effects=True, vmem_limit_bytes=56 * 2**20),
        )(points, labels.reshape(-1, 128), centre_index.reshape(1, -1), kernel_factor, ridge_factor)
        return fitted.reshape(-1)

    whole = ("group", "ctr", "dp")
    in_specs = (P(whole, None), P(whole), P(whole), P(("group", "ctr"), None), P(("group", "ctr"), None))
    return jax.shard_map(body, mesh=mesh, in_specs=in_specs, out_specs=P(whole), check_vma=False)
```

```python
import functools

import jax
import jax.numpy as jnp
from jax import lax
from jax.experimental import pallas as pl
from jax.experimental.pallas import tpu as pltpu
from jax.sharding import PartitionSpec as P

ITERS = 2
RIDGE = 0.001
MESH = pl.DeviceIdType.MESH
F32 = jnp.float32
BF16 = jnp.bfloat16
NT = (((1,), (1,)), ((), ()))


def kernel(nc, nd, flat, pts_in, lab_in, idx_in, kf_in, rf_in, out,
           pts, lab, idx, kf, cbuf, kt, rbuf, tbuf, zbuf, xbuf,
           ins, c1s, c1r, c2s, c2r, fs, fr, zs, zr, xs, xr):
    n_pts, feats = pts.shape
    per = idx.shape[1]
    half = feats // 2
    cb = per * nd
    m = cb * nc
    all_points = float(n_pts * nc * nd)
    c = lax.axis_index("ctr")
    d = lax.axis_index("dp")

    others = [(kc, kd) for kc in range(nc) for kd in range(nd) if kc or kd]
    near = [(kc, kd) for kc, kd in others if not (kc and kd)]
    barrier = pltpu.get_barrier_semaphore()
    for kc, kd in near:
        pl.semaphore_signal(barrier, inc=1, device_id_type=MESH,
                            device_id={"ctr": lax.rem(c + kc, nc), "dp": lax.rem(d + kd, nd)})
    loads = [pltpu.make_async_copy(a, b, ins.at[i]) for i, (a, b) in enumerate(
        ((idx_in, idx), (pts_in, pts), (kf_in, kf), (rf_in, rbuf.at[c]), (lab_in, lab)))]
    for load in loads:
        load.start()

    first = (c * nd + d) * n_pts
    loads[0].wait()
    loads[1].wait()
    local = (idx[...] - first).astype(F32)
    square = lax.broadcasted_iota(jnp.int32, (per, per), 0) == lax.broadcasted_iota(jnp.int32, (per, per), 1)
    local = jnp.sum(jnp.where(square, local, 0.0), axis=1, keepdims=True).astype(jnp.int32)
    places = lax.broadcasted_iota(jnp.int32, (per, n_pts), 1)
    onehot = jnp.where(places == local, 1.0, 0.0).astype(BF16)
    chosen = jnp.dot(onehot, pts[...], preferred_element_type=F32)
    cbuf[c, d] = jnp.concatenate([chosen[:, :half], chosen[:, half:]], axis=0).astype(BF16)

    loads[2].wait()
    tbuf[c] = kf[...].T
    loads[3].wait()
    loads[4].wait()

    pl.semaphore_wait(barrier, len(near))

    def spread(ref_src, axis, me, n, send, recv):
        copies = []
        for k in range(1, n):
            copy = pltpu.make_async_remote_copy(
                src_ref=ref_src, dst_ref=ref_src, send_sem=send.at[k - 1], recv_sem=recv.at[k - 1],
                device_id={axis: lax.rem(me + k, n)}, device_id_type=MESH)
            copy.start()
            copies.append(copy)
        return copies

    sent = []
    first_copies = spread(cbuf.at[c, d], "dp", d, nd, c1s, c1r)
    sent += first_copies

    def factor_copy(which, block, to, send):
        rest = pl.ds(cb * block, m - cb * block)
        ref = rbuf.at[block, :, rest] if which else tbuf.at[block, rest]
        return pltpu.make_async_remote_copy(
            src_ref=ref, dst_ref=ref, send_sem=fs.at[which, send], recv_sem=fr.at[which, block],
            device_id={"ctr": to}, device_id_type=MESH)

    def same_core(cc):
        return [(cc + k) % nc for k in range(2, nc, 2)]

    def direct(cc, which):
        return [factor_copy(which, cc, p, p) for p in same_core(cc) + [cc ^ 1]]

    def handed(cc, which):
        return [factor_copy(which, p, cc ^ 1, nc + p) for p in same_core(cc)]

    def arriving(cc, which):
        return [factor_copy(which, p, p, p) for p in same_core(cc ^ 1) + [cc ^ 1]]

    def on_each(action):
        for cc in range(nc):
            pl.when(c == cc)(functools.partial(action, cc))

    def factors_start(which, cc):
        for copy in direct(cc, which):
            copy.start()

    def factors_hand_on(which, cc):
        for p in same_core(cc):
            factor_copy(which, p, p, p).wait_recv()
        for copy in handed(cc, which):
            copy.start()

    def factors_arrive(which, cc):
        for copy in arriving(cc, which):
            copy.wait_recv()

    def factors_end(cc):
        for which in range(2):
            for copy in direct(cc, which) + handed(cc, which):
                copy.wait_send()

    on_each(functools.partial(factors_start, 0))
    wide = pts[...].astype(F32)
    sq = wide * wide
    sq_hi = sq.astype(BF16)
    sq_lo = (sq - sq_hi.astype(F32)).astype(BF16)
    ones = jnp.ones((8, feats), BF16)
    point_sq = (lax.dot_general(ones, sq_hi, NT, preferred_element_type=F32)
                + lax.dot_general(ones, sq_lo, NT, preferred_element_type=F32))[:1]

    for copy in first_copies:
        copy.wait_recv()
    second_copies = spread(cbuf.at[c], "ctr", c, nc, c2s, c2r)
    sent += second_copies

    on_each(functools.partial(factors_start, 1))

    def form(owner):
        block = cbuf[owner].astype(F32).reshape(nd, 2, per, half)
        left = block[:, 0].reshape(cb, half)
        right = block[:, 1].reshape(cb, half)
        centre_sq = jnp.sum(left * left + right * right, axis=1, keepdims=True)
        centres = jnp.concatenate([left, right], axis=1).astype(BF16)
        products = lax.dot_general(centres, pts[...], NT, preferred_element_type=F32)
        exponent = (2.0 * products - point_sq - centre_sq) * (2.0 / feats)
        kt[pl.ds(pl.multiple_of(owner * cb, cb), cb), :] = jnp.exp(exponent).astype(BF16)

    form(c)
    on_each(functools.partial(factors_hand_on, 0))
    for k in range(1, nc):
        second_copies[k - 1].wait_recv()
        form(lax.rem(c - k + nc, nc))

    def total(r, part, meanwhile=None):
        if flat:
            zbuf[r, c, d] = part
            copies = []
            for i, (kc, kd) in enumerate(others):
                copy = pltpu.make_async_remote_copy(
                    src_ref=zbuf.at[r, c, d], dst_ref=zbuf.at[r, c, d],
                    send_sem=zs.at[r, i], recv_sem=zr.at[r, i], device_id_type=MESH,
                    device_id={"ctr": lax.rem(c + kc, nc), "dp": lax.rem(d + kd, nd)})
                copy.start()
                copies.append(copy)
            if meanwhile is not None:
                meanwhile()
            for copy in copies:
                copy.wait_recv()
            sent.extend(copies)
            return jnp.sum(zbuf[r].reshape(nc * nd, m), axis=0, keepdims=True)
        zbuf[r, 0, d] = part
        copies = spread(zbuf.at[r, 0, d], "dp", d, nd, zs.at[r], zr.at[r])
        for copy in copies:
            copy.wait_recv()
        xbuf[r, c] = jnp.sum(zbuf[r, 0].reshape(nd, m), axis=0, keepdims=True)
        more = spread(xbuf.at[r, c], "ctr", c, nc, xs.at[r], xr.at[r])
        if meanwhile is not None:
            meanwhile()
        for copy in more:
            copy.wait_recv()
        sent.extend(copies + more)
        return jnp.sum(xbuf[r].reshape(nc, m), axis=0, keepdims=True)

    def ridge_solve(row):
        return [jnp.sum(rbuf[b, :, cb * b:] * row[:, cb * b:], axis=1, keepdims=True) for b in range(nc)]

    def ridge_solve_transposed(column):
        parts = [0.0] * nc
        for b in range(nc):
            for j in range(b, nc):
                prod = rbuf[b, :, cb * j:cb * (j + 1)] * column[b]
                parts[j] = parts[j] + prod
        return jnp.concatenate([jnp.sum(p, axis=0, keepdims=True) for p in parts], axis=1)

    def kernel_solve(column):
        rows = []
        for b in range(nc):
            acc = 0.0
            for j in range(b, nc):
                acc = acc + tbuf[b, cb * j:cb * (j + 1), :] * column[j]
            rows.append(jnp.sum(acc, axis=0, keepdims=True))
        return jnp.concatenate(rows, axis=1)

    def kernel_solve_transposed(row):
        columns = []
        for j in range(nc):
            acc = 0.0
            for b in range(j + 1):
                acc = acc + tbuf[b, cb * j:cb * (j + 1), :] * row[:, cb * b:cb * (b + 1)]
            columns.append(jnp.sum(acc, axis=1, keepdims=True))
        return columns

    def to_centres(row):
        return lax.dot_general(row, kt[...], NT, preferred_element_type=F32)

    def to_points(row):
        return jnp.dot(row, kt[...], preferred_element_type=F32)

    label_row = jnp.concatenate([lab[r:r + 1, :] for r in range(n_pts // 128)], axis=1)
    summed = total(0, to_centres(label_row), lambda: on_each(functools.partial(factors_hand_on, 1)))
    on_each(functools.partial(factors_arrive, 0))
    lowered = kernel_solve_transposed(summed / all_points)
    on_each(functools.partial(factors_arrive, 1))
    right_side = ridge_solve_transposed(lowered)
    beta = jnp.zeros_like(right_side)
    residual = right_side
    direction = right_side
    norm_now = jnp.sum(residual * residual, axis=1, keepdims=True)
    for iteration in range(ITERS):
        scaled = ridge_solve(direction)
        lifted = kernel_solve(scaled).astype(BF16)
        image = to_points(lifted).astype(BF16)
        summed = total(1 + iteration, to_centres(image))
        inner = kernel_solve_transposed(summed / all_points)
        mapped = ridge_solve_transposed([a + RIDGE * s for a, s in zip(inner, scaled)])
        step = norm_now / jnp.sum(direction * mapped, axis=1, keepdims=True)
        beta = beta + step * direction
        residual = residual - step * mapped
        norm_next = jnp.sum(residual * residual, axis=1, keepdims=True)
        direction = residual + (norm_next / norm_now) * direction
        norm_now = norm_next
    coefficients = kernel_solve(ridge_solve(beta)).astype(BF16)
    out[...] = to_points(coefficients)

    for copy in sent:
        copy.wait_send()
    on_each(factors_end)


def solution(mesh):
    nc, nd = mesh.shape["ctr"], mesh.shape["dp"]

    def body(points, labels, centre_index, kernel_factor, ridge_factor):
        n_pts, feats = points.shape
        per = centre_index.shape[0]
        cb = kernel_factor.shape[0]
        m = cb * nc
        dma = pltpu.SemaphoreType.DMA
        rounds = ITERS + 1
        flat = nc * nd <= 32
        rows = nc if flat else 1
        links = nc * nd - 1 if flat else nd - 1
        fitted = pl.pallas_call(
            functools.partial(kernel, nc, nd, flat),
            out_shape=jax.ShapeDtypeStruct((1, n_pts), F32),
            in_specs=[pl.BlockSpec(memory_space=pl.ANY)] * 5,
            out_specs=pl.BlockSpec(memory_space=pltpu.VMEM),
            scratch_shapes=[
                pltpu.VMEM((n_pts, feats), BF16),
                pltpu.VMEM((n_pts // 128, 128), BF16),
                pltpu.VMEM((1, per), jnp.int32),
                pltpu.VMEM((cb, m), F32),
                pltpu.VMEM((nc, nd, 2 * per, feats // 2), BF16),
                pltpu.VMEM((m, n_pts), BF16),
                pltpu.VMEM((nc, cb, m), F32),
                pltpu.VMEM((nc, m, cb), F32),
                pltpu.VMEM((rounds, rows, nd, 1, m), F32),
                pltpu.VMEM((rounds, nc, 1, m), F32),
                dma((5,)),
                dma((nd - 1,)), dma((nd - 1,)),
                dma((nc - 1,)), dma((nc - 1,)),
                dma((2, 2 * nc)), dma((2, nc)),
                dma((rounds, links)), dma((rounds, links)),
                dma((rounds, nc - 1)), dma((rounds, nc - 1)),
            ],
            compiler_params=pltpu.CompilerParams(
                collective_id=0, has_side_effects=True, vmem_limit_bytes=56 * 2**20),
        )(points, labels.reshape(-1, 128), centre_index.reshape(1, -1), kernel_factor, ridge_factor)
        return fitted.reshape(-1)

    whole = ("group", "ctr", "dp")
    in_specs = (P(whole, None), P(whole), P(whole), P(("group", "ctr"), None), P(("group", "ctr"), None))
    return jax.shard_map(body, mesh=mesh, in_specs=in_specs, out_specs=P(whole), check_vma=False)
```

```python
import functools

import jax
import jax.numpy as jnp
from jax import lax
from jax.experimental import pallas as pl
from jax.experimental.pallas import tpu as pltpu
from jax.sharding import PartitionSpec as P

ITERS = 2
RIDGE = 0.001
MESH = pl.DeviceIdType.MESH
F32 = jnp.float32
BF16 = jnp.bfloat16
NT = (((1,), (1,)), ((), ()))


def kernel(nc, nd, flat, pts_in, lab_in, idx_in, kf_in, rf_in, out,
           pts, lab, idx, kf, cbuf, kt, rbuf, tbuf, zbuf, xbuf,
           ins, c1s, c1r, c2s, c2r, fs, fr, zs, zr, xs, xr):
    n_pts, feats = pts.shape
    per = idx.shape[1]
    half = feats // 2
    cb = per * nd
    m = cb * nc
    all_points = float(n_pts * nc * nd)
    c = lax.axis_index("ctr")
    d = lax.axis_index("dp")

    others = [(kc, kd) for kc in range(nc) for kd in range(nd) if kc or kd]
    near = [(kc, kd) for kc, kd in others if not (kc and kd)]
    barrier = pltpu.get_barrier_semaphore()
    for kc, kd in near:
        pl.semaphore_signal(barrier, inc=1, device_id_type=MESH,
                            device_id={"ctr": lax.rem(c + kc, nc), "dp": lax.rem(d + kd, nd)})
    loads = [pltpu.make_async_copy(a, b, ins.at[i]) for i, (a, b) in enumerate(
        ((idx_in, idx), (pts_in, pts), (kf_in, kf), (rf_in, rbuf.at[c]), (lab_in, lab)))]
    for load in loads:
        load.start()

    first = (c * nd + d) * n_pts
    loads[0].wait()
    loads[1].wait()
    local = (idx[...] - first).astype(F32)
    square = lax.broadcasted_iota(jnp.int32, (per, per), 0) == lax.broadcasted_iota(jnp.int32, (per, per), 1)
    local = jnp.sum(jnp.where(square, local, 0.0), axis=1, keepdims=True).astype(jnp.int32)
    places = lax.broadcasted_iota(jnp.int32, (per, n_pts), 1)
    onehot = jnp.where(places == local, 1.0, 0.0).astype(BF16)
    chosen = jnp.dot(onehot, pts[...], preferred_element_type=F32)
    cbuf[c, d] = jnp.concatenate([chosen[:, :half], chosen[:, half:]], axis=0).astype(BF16)

    loads[2].wait()
    tbuf[c] = kf[...].T
    loads[3].wait()
    loads[4].wait()

    pl.semaphore_wait(barrier, len(near))

    def spread(ref_src, axis, me, n, send, recv):
        copies = []
        for k in range(1, n):
            copy = pltpu.make_async_remote_copy(
                src_ref=ref_src, dst_ref=ref_src, send_sem=send.at[k - 1], recv_sem=recv.at[k - 1],
                device_id={axis: lax.rem(me + k, n)}, device_id_type=MESH)
            copy.start()
            copies.append(copy)
        return copies

    sent = []
    first_copies = spread(cbuf.at[c, d], "dp", d, nd, c1s, c1r)
    sent += first_copies

    def factor_copy(which, block, to, send):
        rest = pl.ds(cb * block, m - cb * block)
        ref = rbuf.at[block, :, rest] if which else tbuf.at[block, rest]
        return pltpu.make_async_remote_copy(
            src_ref=ref, dst_ref=ref, send_sem=fs.at[which, send], recv_sem=fr.at[which, block],
            device_id={"ctr": to}, device_id_type=MESH)

    def same_core(cc):
        return [(cc + k) % nc for k in range(2, nc, 2)]

    def direct(cc, which):
        return [factor_copy(which, cc, p, p) for p in same_core(cc) + [cc ^ 1]]

    def handed(cc, which):
        return [factor_copy(which, p, cc ^ 1, nc + p) for p in same_core(cc)]

    def arriving(cc, which):
        return [factor_copy(which, p, p, p) for p in same_core(cc ^ 1) + [cc ^ 1]]

    def on_each(action):
        for cc in range(nc):
            pl.when(c == cc)(functools.partial(action, cc))

    def factors_start(which, cc):
        for copy in direct(cc, which):
            copy.start()

    def factors_hand_on(which, cc):
        for p in same_core(cc):
            factor_copy(which, p, p, p).wait_recv()
        for copy in handed(cc, which):
            copy.start()

    def factors_arrive(which, cc):
        for copy in arriving(cc, which):
            copy.wait_recv()

    def factors_end(cc):
        for which in range(2):
            for copy in direct(cc, which) + handed(cc, which):
                copy.wait_send()

    on_each(functools.partial(factors_start, 0))
    wide = pts[...].astype(F32)
    sq = wide * wide
    sq_hi = sq.astype(BF16)
    sq_lo = (sq - sq_hi.astype(F32)).astype(BF16)
    ones = jnp.ones((8, feats), BF16)
    point_sq = (lax.dot_general(ones, sq_hi, NT, preferred_element_type=F32)
                + lax.dot_general(ones, sq_lo, NT, preferred_element_type=F32))[:1]

    for copy in first_copies:
        copy.wait_recv()
    second_copies = spread(cbuf.at[c], "ctr", c, nc, c2s, c2r)
    sent += second_copies

    on_each(functools.partial(factors_start, 1))

    def form(owner):
        block = cbuf[owner].astype(F32).reshape(nd, 2, per, half)
        left = block[:, 0].reshape(cb, half)
        right = block[:, 1].reshape(cb, half)
        centre_sq = jnp.sum(left * left + right * right, axis=1, keepdims=True)
        centres = jnp.concatenate([left, right], axis=1).astype(BF16)
        products = lax.dot_general(centres, pts[...], NT, preferred_element_type=F32)
        exponent = (2.0 * products - point_sq - centre_sq) * (2.0 / feats)
        kt[pl.ds(pl.multiple_of(owner * cb, cb), cb), :] = jnp.exp(exponent).astype(BF16)

    form(c)
    on_each(functools.partial(factors_hand_on, 0))
    for k in range(1, nc):
        second_copies[k - 1].wait_recv()
        form(lax.rem(c - k + nc, nc))

    def total(r, part, meanwhile=None):
        if flat:
            zbuf[r, c, d] = part
            copies = []
            for i, (kc, kd) in enumerate(others):
                copy = pltpu.make_async_remote_copy(
                    src_ref=zbuf.at[r, c, d], dst_ref=zbuf.at[r, c, d],
                    send_sem=zs.at[r, i], recv_sem=zr.at[r, i], device_id_type=MESH,
                    device_id={"ctr": lax.rem(c + kc, nc), "dp": lax.rem(d + kd, nd)})
                copy.start()
                copies.append(copy)
            if meanwhile is not None:
                meanwhile()
            for copy in copies:
                copy.wait_recv()
            sent.extend(copies)
            return jnp.sum(zbuf[r].reshape(nc * nd, m), axis=0, keepdims=True)
        zbuf[r, 0, d] = part
        copies = spread(zbuf.at[r, 0, d], "dp", d, nd, zs.at[r], zr.at[r])
        for copy in copies:
            copy.wait_recv()
        xbuf[r, c] = jnp.sum(zbuf[r, 0].reshape(nd, m), axis=0, keepdims=True)
        more = spread(xbuf.at[r, c], "ctr", c, nc, xs.at[r], xr.at[r])
        if meanwhile is not None:
            meanwhile()
        for copy in more:
            copy.wait_recv()
        sent.extend(copies + more)
        return jnp.sum(xbuf[r].reshape(nc, m), axis=0, keepdims=True)

    def ridge_solve(row):
        return [jnp.sum(rbuf[b, :, cb * b:] * row[:, cb * b:], axis=1, keepdims=True) for b in range(nc)]

    def ridge_solve_transposed(column):
        parts = [0.0] * nc
        for b in range(nc):
            for j in range(b, nc):
                prod = rbuf[b, :, cb * j:cb * (j + 1)] * column[b]
                parts[j] = parts[j] + prod
        return jnp.concatenate([jnp.sum(p, axis=0, keepdims=True) for p in parts], axis=1)

    def kernel_solve(column):
        rows = []
        for b in range(nc):
            acc = 0.0
            for j in range(b, nc):
                acc = acc + tbuf[b, cb * j:cb * (j + 1), :] * column[j]
            rows.append(jnp.sum(acc, axis=0, keepdims=True))
        return jnp.concatenate(rows, axis=1)

    def kernel_solve_transposed(row):
        columns = []
        for j in range(nc):
            acc = 0.0
            for b in range(j + 1):
                acc = acc + tbuf[b, cb * j:cb * (j + 1), :] * row[:, cb * b:cb * (b + 1)]
            columns.append(jnp.sum(acc, axis=1, keepdims=True))
        return columns

    def to_centres(row):
        return lax.dot_general(row, kt[...], NT, preferred_element_type=F32)

    def to_points(row):
        return jnp.dot(row, kt[...], preferred_element_type=F32)

    label_row = jnp.concatenate([lab[r:r + 1, :] for r in range(n_pts // 128)], axis=1)
    summed = total(0, to_centres(label_row), lambda: on_each(functools.partial(factors_hand_on, 1)))
    on_each(functools.partial(factors_arrive, 0))
    lowered = kernel_solve_transposed(summed / all_points)
    on_each(functools.partial(factors_arrive, 1))
    right_side = ridge_solve_transposed(lowered)
    solved = 0.0
    residual = right_side
    direction = right_side
    norm_now = jnp.sum(residual * residual, axis=1, keepdims=True)
    for iteration in range(ITERS):
        scaled = ridge_solve(direction)
        lifted = kernel_solve(scaled)
        image = to_points(lifted.astype(BF16)).astype(BF16)
        weighed = to_centres(image)
        if iteration == ITERS - 1:
            length = sum(jnp.sum(s * s, axis=0, keepdims=True) for s in scaled)
            shared = jnp.sum(total(1 + iteration, lifted * weighed), axis=1, keepdims=True)
            solved = solved + (norm_now / (shared / all_points + RIDGE * length)) * lifted
            break
        summed = total(1 + iteration, weighed)
        inner = kernel_solve_transposed(summed / all_points)
        mapped = ridge_solve_transposed([a + RIDGE * s for a, s in zip(inner, scaled)])
        step = norm_now / jnp.sum(direction * mapped, axis=1, keepdims=True)
        solved = solved + step * lifted
        residual = residual - step * mapped
        norm_next = jnp.sum(residual * residual, axis=1, keepdims=True)
        direction = residual + (norm_next / norm_now) * direction
        norm_now = norm_next
    out[...] = to_points(solved.astype(BF16))

    for copy in sent:
        copy.wait_send()
    on_each(factors_end)


def solution(mesh):
    nc, nd = mesh.shape["ctr"], mesh.shape["dp"]

    def body(points, labels, centre_index, kernel_factor, ridge_factor):
        n_pts, feats = points.shape
        per = centre_index.shape[0]
        cb = kernel_factor.shape[0]
        m = cb * nc
        dma = pltpu.SemaphoreType.DMA
        rounds = ITERS + 1
        flat = nc * nd <= 32
        rows = nc if flat else 1
        links = nc * nd - 1 if flat else nd - 1
        fitted = pl.pallas_call(
            functools.partial(kernel, nc, nd, flat),
            out_shape=jax.ShapeDtypeStruct((1, n_pts), F32),
            in_specs=[pl.BlockSpec(memory_space=pl.ANY)] * 5,
            out_specs=pl.BlockSpec(memory_space=pltpu.VMEM),
            scratch_shapes=[
                pltpu.VMEM((n_pts, feats), BF16),
                pltpu.VMEM((n_pts // 128, 128), BF16),
                pltpu.VMEM((1, per), jnp.int32),
                pltpu.VMEM((cb, m), F32),
                pltpu.VMEM((nc, nd, 2 * per, feats // 2), BF16),
                pltpu.VMEM((m, n_pts), BF16),
                pltpu.VMEM((nc, cb, m), F32),
                pltpu.VMEM((nc, m, cb), F32),
                pltpu.VMEM((rounds, rows, nd, 1, m), F32),
                pltpu.VMEM((rounds, nc, 1, m), F32),
                dma((5,)),
                dma((nd - 1,)), dma((nd - 1,)),
                dma((nc - 1,)), dma((nc - 1,)),
                dma((2, 2 * nc)), dma((2, nc)),
                dma((rounds, links)), dma((rounds, links)),
                dma((rounds, nc - 1)), dma((rounds, nc - 1)),
            ],
            compiler_params=pltpu.CompilerParams(
                collective_id=0, has_side_effects=True, vmem_limit_bytes=56 * 2**20),
        )(points, labels.reshape(-1, 128), centre_index.reshape(1, -1), kernel_factor, ridge_factor)
        return fitted.reshape(-1)

    whole = ("group", "ctr", "dp")
    in_specs = (P(whole, None), P(whole), P(whole), P(("group", "ctr"), None), P(("group", "ctr"), None))
    return jax.shard_map(body, mesh=mesh, in_specs=in_specs, out_specs=P(whole), check_vma=False)
```
